32 devices in a mesh: seq: 8 (over y, x, core), ew: 4 (over z).
Axes of the slice: x: 2, y: 2, z: 4, core: 2. Of those that a mesh axis runs over, the one named last changes fastest.
Arguments:
- tokens: bfloat16 [2048, 4096], P('seq', 'ew'), may hold values from -6 to 6
- cotangent: bfloat16 [2048, 4096], P('seq', 'ew'), may hold values from -6 to 6
- w_in: bfloat16 [16384, 4096], P(('seq', 'ew')), may hold values from -0.1875 to 0.1875
- w_out: bfloat16 [16384, 4096], P(('seq', 'ew')), may hold values from -0.1875 to 0.1875
- bar_picks: int32 [4, 256], replicated, may hold values from 0 to 2047, as said below
- gate_weights: float32 [4, 256], replicated, may hold values from 0.2 to 1
Outputs:
- moe_out: bfloat16 [2048, 4096], P('seq', 'ew')
- token_gradient: bfloat16 [2048, 4096], P('seq', 'ew')
The draws below stay inside these ranges and needn't reach their ends.
Inputs may be any that keep to these rules, and one draw needn't show every extreme that they name: `bar_picks`: each row lists 256 distinct bar tokens. At most 64 of one row's entries lie in one aligned block of 256 bars (the bars of one index of seq), and every row has exactly 64 entries in some block.
All inputs are finite; a program needn't handle non-finite values.
Results may differ from the reference program's by a relative error of at most 0.013.
Values may be sent and summed in bfloat16 or wider, within the bound.
A program may use at most 64 MiB of HBM per device.

```python
import math
import jax
import jax.numpy as jnp
from jax import lax

D = 4096
FF = 4096
TOK_DEV = 256
EXPERTS = 4
CAP = 256
MOST = 64
FF_DEV = 512
TOKENS = 2048
N_SEQ = 8


def draw_bar_picks(key, part):
    key = jax.random.fold_in(key, 7)
    shards = TOKENS // TOK_DEV
    subkeys = jax.random.split(key, 5)
    popular = jax.random.randint(subkeys[0], (shards,), 0, 4)
    jitter = jax.random.randint(subkeys[1], (EXPERTS, shards), 0, 64)
    scores = (popular[None, :] * 64 + jitter) * shards + jnp.arange(shards, dtype=jnp.int32)[None, :]
    visit_order = jnp.argsort(-scores, axis=1)
    unit_draws = jax.random.randint(subkeys[2], (EXPERTS, shards), 0, 1 << 20)

    def fill(remain, inputs):
        position, unit_draw = inputs
        shards_left = shards - 1 - position
        lowest = jnp.maximum(0, remain - shards_left * MOST)
        highest = jnp.minimum(MOST, remain)
        how_many = lowest + unit_draw % (highest - lowest + 1)
        how_many = jnp.where(position == 0, MOST, how_many)
        return (remain - how_many, how_many)
    initial = jnp.full((EXPERTS,), CAP, jnp.int32)
    remain_end, taken_counts = lax.scan(fill, initial, (jnp.arange(shards, dtype=jnp.int32), unit_draws.T))
    taken_counts = taken_counts.T
    counts = jnp.zeros((EXPERTS, shards), jnp.int32).at[jnp.arange(EXPERTS)[:, None], visit_order].set(taken_counts)
    spot_noise = jax.random.randint(subkeys[3], (EXPERTS, shards, TOK_DEV), 0, 1 << 16)
    spot_ids = jnp.argsort(spot_noise * TOK_DEV + jnp.arange(TOK_DEV, dtype=jnp.int32), axis=2)[:, :, :MOST]
    candidate_tokens = spot_ids + (jnp.arange(shards, dtype=jnp.int32) * TOK_DEV)[None, :, None]
    valid_mask = jnp.arange(MOST)[None, None, :] < counts[:, :, None]
    flat_ids = candidate_tokens.reshape(EXPERTS, shards * MOST)
    ranked = jnp.argsort(jnp.where(valid_mask, 0, 1).reshape(EXPERTS, shards * MOST), axis=1, stable=True)[:, :CAP]
    chosen = jnp.take_along_axis(flat_ids, ranked, axis=1)
    mixing = jax.random.randint(subkeys[4], (EXPERTS, CAP), 0, 1 << 16)
    shuffle = jnp.argsort(mixing * CAP + jnp.arange(CAP, dtype=jnp.int32), axis=1)
    return jnp.take_along_axis(chosen, shuffle, axis=1).astype(jnp.int32)


def spiked(result, key, source, target, blocks, factor):
    def block_of(dim):
        return (jnp.arange(result.shape[dim]) // (result.shape[dim] // blocks)).reshape((-1,) + (1,) * (result.ndim - 1 - dim))

    near = jax.random.permutation(key, blocks)[block_of(target)]
    other_side = (block_of(target) + blocks // 2) % blocks
    return jnp.where((block_of(source) == near) | (block_of(source) == other_side), factor * result, result)


def block_scale(rng, dims, cuts, low, top_value):
    level, own = 1.0, jax.random.fold_in(rng, 6)
    for axis_at, shards_of in cuts:
        steps = jnp.exp(jax.random.uniform(jax.random.fold_in(own, axis_at), (shards_of,), jnp.float32, low / len(cuts), top_value / len(cuts)))
        level = level * jnp.repeat(steps, dims[axis_at] // shards_of).reshape([-1 if axis == axis_at else 1 for axis in range(len(dims))])
    return level


def scatter_about(key, shape, deviation, reach, cuts=(), kind=jnp.bfloat16):
    entries = jax.random.normal(key, shape, jnp.float32) * deviation
    if len(cuts) > 0:
        entries = block_scale(key, shape, cuts, -0.22, 0.18) * entries
    return jnp.clip(entries, min=-reach, max=reach).astype(kind)


def noise_with(key, dims, width, bound, cuts, heavy, kind=jnp.bfloat16):
    array = width * jax.random.normal(key, dims, jnp.float32)
    if cuts:
        array = array * block_scale(key, dims, cuts, -0.22, 0.18)
    return jnp.clip(spiked(array, jax.random.fold_in(key, 3), *heavy), -bound, bound).astype(kind)


def setup_inputs(seed: int = 0) -> dict:
    key_list = jax.random.split(jax.random.key(seed), 7)
    return {
        "tokens": scatter_about(key_list[0], (TOKENS, D), 1.0, 6.0, ((0, 8), (1, 4))),
        "cotangent": scatter_about(key_list[1], (TOKENS, D), 1.0, 6.0, ((0, 8), (1, 4))),
        "w_in": noise_with(key_list[2], (EXPERTS * FF, D), D ** -0.5, 0.1875, ((0, 32),), (0, 1, 32, 2.75)),
        "w_out": noise_with(key_list[3], (EXPERTS * FF, D), FF ** -0.5, 0.1875, ((0, 32),), (0, 1, 32, 2.75)),
        "bar_picks": draw_bar_picks(jax.random.fold_in(key_list[6], 71), 0),
        "gate_weights": jnp.clip(jnp.exp(jax.random.uniform(key_list[5], (EXPERTS, CAP), jnp.float32, math.log(0.2), math.log(1.0))), 0.2, 1.0),
    }


def smooth(values):
    return jax.nn.gelu(values, approximate=False)

def blockwise(leftward_half, right_side, blocks):
    row_count = leftward_half.shape[0]
    block_width = leftward_half.shape[1] // blocks
    leftward_blocks = leftward_half.reshape(row_count, blocks, block_width).astype(jnp.float32)
    rightward_blocks = right_side.reshape(blocks, block_width, right_side.shape[1]).astype(jnp.float32)
    partial_sums = jnp.einsum('gjy,jyq->jgq', leftward_blocks, rightward_blocks)
    partial_sums = lax.optimization_barrier(partial_sums.astype(jnp.bfloat16))
    return partial_sums.astype(jnp.float32)

def reference(tokens, cotangent, w_in, w_out, bar_picks, gate_weights):
    halves = N_SEQ // EXPERTS
    blocks = FF // FF_DEV
    stacked_in = w_in.reshape(EXPERTS, FF, D)
    stacked_out = w_out.reshape(EXPERTS, FF, D)

    def one_expert(carry, inputs):
        out_sum, grad_sum = carry
        picked, weight_in, weight_out, gate_row = inputs
        rows_tok = tokens[picked]
        rows_grad = cotangent[picked]
        hidden = jnp.dot(rows_tok, weight_in.T, preferred_element_type=jnp.float32)
        activated, pull_back = jax.vjp(smooth, hidden)
        slope_in = jnp.dot(rows_grad, weight_out.T, preferred_element_type=jnp.float32)
        back_hidden = pull_back(slope_in)[0].astype(jnp.bfloat16)
        act_bf16 = activated.astype(jnp.bfloat16)
        part_out = blockwise(act_bf16, weight_out, blocks)
        part_grad = blockwise(back_hidden, weight_in, blocks)
        half_out = lax.optimization_barrier(jnp.sum(part_out.reshape(halves, blocks // halves, CAP, D), axis=1))
        half_grad = lax.optimization_barrier(jnp.sum(part_grad.reshape(halves, blocks // halves, CAP, D), axis=1))
        term_out = lax.optimization_barrier(jnp.sum(gate_row[None, :, None] * half_out, axis=0))
        term_grad = lax.optimization_barrier(jnp.sum(gate_row[None, :, None] * half_grad, axis=0))
        return ((out_sum.at[picked].add(term_out), grad_sum.at[picked].add(term_grad)), None)
    initial = (jnp.zeros((TOKENS, D), jnp.float32), jnp.zeros((TOKENS, D), jnp.float32))
    (out_sum, grad_sum), unused = lax.scan(one_expert, initial, (bar_picks, stacked_in, stacked_out, gate_weights))
    return (out_sum.astype(jnp.bfloat16), grad_sum.astype(jnp.bfloat16))
```

```python
import functools
import math

import jax
import jax.numpy as jnp
from jax import lax
from jax.experimental import pallas as pl
from jax.experimental.pallas import tpu as pltpu
from jax.sharding import PartitionSpec as P

MESH = pl.DeviceIdType.MESH
F32 = jnp.float32
BF16 = jnp.bfloat16


def iota(shape, dim):
    return lax.broadcasted_iota(jnp.int32, shape, dim).astype(F32)


def to_column(row):
    n = row.shape[1]
    return jnp.sum(jnp.where(iota((n, n), 0) == iota((n, n), 1), row, 0.0), axis=1, keepdims=True)


def to_row(col):
    n = col.shape[0]
    return jnp.sum(jnp.where(iota((n, n), 0) == iota((n, n), 1), col, 0.0), axis=0, keepdims=True)


def dot(a, b, dims=(1, 0)):
    return lax.dot_general(
        a, b, (((dims[0],), (dims[1],)), ((), ())), preferred_element_type=F32
    )


def kernel(
    rows, n_seq, n_ew,
    tok_ref, cot_ref, win_ref, wout_ref, picks_ref, gates_ref,
    out_ref, grad_ref,
    wv, pk, uu, gcol, send, recv, full, hid, slo, hb, px, own, xch,
    ard, aru, sdn, sup, total, bsend, home,
    wsem, as_, ar_, ps_, pr_, gds, gdr, gus, gur, xs_, xr_, rds, rdr, rus, rur, bs_, br_,
):
    me = lax.axis_index("seq")
    z = lax.axis_index("ew")
    k = lax.rem(me, 2)
    e_me = lax.div(me, 2)
    partner = me + 1 - 2 * k
    experts, cap = picks_ref.shape
    tok, feat = tok_ref.shape
    slots = send.shape[3]
    starts = [sum(rows[:r]) for r in range(2)]
    last = n_ew - 1
    span = [pl.ds(starts[r], rows[r]) for r in range(2)]

    barrier = pltpu.get_barrier_semaphore()
    for i in range(1, n_seq):
        pl.semaphore_signal(
            barrier, inc=1, device_id=(lax.rem(me + i, n_seq), z), device_id_type=MESH
        )

    @pl.when(z > 0)
    def _():
        pl.semaphore_signal(barrier, inc=1, device_id=(me, z - 1), device_id_type=MESH)

    @pl.when(z < last)
    def _():
        pl.semaphore_signal(barrier, inc=1, device_id=(me, z + 1), device_id_type=MESH)

    w_copies = [
        pltpu.make_async_copy(wout_ref, wv.at[0], wsem.at[0]),
        pltpu.make_async_copy(win_ref, wv.at[1], wsem.at[1]),
    ]
    for c in w_copies:
        c.start()

    base = (me * tok).astype(F32)
    t_col = iota((tok, cap), 0) + base
    for e in range(experts):
        pick = picks_ref[e : e + 1, :].astype(F32)
        hit = jnp.sum(jnp.where(pick == t_col, 1.0, 0.0), axis=1, keepdims=True)
        rank = jnp.sum(
            jnp.where((pick >= base) & (pick < t_col), 1.0, 0.0), axis=1, keepdims=True
        )
        key = to_row(jnp.where(hit > 0.0, rank, -1.0))
        for r in range(2):
            want = 2.0 * iota((slots, tok), 0) + float(r)
            pk[r, e] = jnp.where(want == key, 1.0, 0.0).astype(BF16)

    inside = (z > 0) & (z < last)

    @pl.when(inside)
    def _():
        pl.semaphore_wait(barrier, n_seq + 1)

    @pl.when(jnp.logical_not(inside))
    def _():
        pl.semaphore_wait(barrier, n_seq)

    def remote(src, dst, s, r, dev):
        return pltpu.make_async_remote_copy(
            src_ref=src, dst_ref=dst, send_sem=s, recv_sem=r, device_id=dev, device_id_type=MESH
        )

    def dispatch(r, i):
        d = lax.rem(me + i, n_seq)
        return remote(
            send.at[r, lax.rem(d, 2), lax.div(d, 2)], recv.at[r, me],
            as_.at[r, i], ar_.at[r, i], (d, z),
        )

    for r in range(2):
        sel = pk[r].reshape(experts * slots, tok)
        send[r, 0] = dot(sel, tok_ref[...]).astype(BF16).reshape(experts, slots, feat)
        send[r, 1] = dot(sel, cot_ref[...]).astype(BF16).reshape(experts, slots, feat)
        for i in range(1, n_seq):
            dispatch(r, i).start()
        recv[r, me] = send[r, k, e_me]

    pick = picks_ref[pl.ds(e_me, 1), :].astype(F32)
    gate = to_column(gates_ref[pl.ds(e_me, 1), :])
    pick_c = to_column(pick)
    owner = jnp.floor((pick + 0.5) * (1.0 / tok))
    owner_c = jnp.floor((pick_c + 0.5) * (1.0 / tok))
    rank_c = jnp.sum(
        jnp.where((owner == owner_c) & (pick < pick_c), 1.0, 0.0), axis=1, keepdims=True
    )
    half_c = jnp.floor(rank_c * 0.5)
    slot_c = owner_c * float(slots) + half_c
    parity = rank_c - 2.0 * half_c
    wide = n_seq * slots
    before = jnp.where(iota((wide, wide), 0) < iota((wide, wide), 1), 1.0, 0.0).astype(BF16)
    for r in range(2):
        here = jnp.where(parity == float(r), slot_c, -1.0)
        match = here == iota((cap, wide), 1)
        valid = jnp.sum(jnp.where(match, 1.0, 0.0), axis=0, keepdims=True)
        gate_pad = jnp.sum(jnp.where(match, gate, 0.0), axis=0, keepdims=True)
        place = dot(jnp.broadcast_to(valid, (16, wide)).astype(BF16), before)[0:1]
        place = jnp.where(valid > 0.0, place, -1.0)
        pick_out = iota((rows[r], wide), 0) == place
        uu[span[r], :] = jnp.where(pick_out, 1.0, 0.0).astype(BF16)
        gcol[span[r], :] = jnp.sum(jnp.where(pick_out, gate_pad, 0.0), axis=1, keepdims=True)

    def compact(r):
        for i in range(1, n_seq):
            dispatch(r, i).wait_recv()
        full[k, z, span[r], :] = dot(
            uu[span[r], :], recv[r].reshape(wide, feat)
        ).astype(BF16)

    def g_down(r, h):
        ref = full.at[k, z + h, span[r]]
        return remote(ref, ref, gds.at[r, h], gdr.at[r, h], (me, z - 1))

    def g_up(r, h):
        ref = full.at[k, z - h, span[r]]
        return remote(ref, ref, gus.at[r, h], gur.at[r, h], (me, z + 1))

    def g_down_in(r, h):
        ref = full.at[k, z + 1 + h, span[r]]
        return remote(ref, ref, gds.at[r, h], gdr.at[r, h], (me, z + 1))

    def g_up_in(r, h):
        ref = full.at[k, z - 1 - h, span[r]]
        return remote(ref, ref, gus.at[r, h], gur.at[r, h], (me, z - 1))

    def g_pair(r, s, i, arr):
        ref = full.at[arr, s, span[r]]
        return remote(ref, ref, ps_.at[r, i], pr_.at[r, i], (partner, z))

    def gather_start(r):
        @pl.when(z > 0)
        def _():
            g_down(r, 0).start()

        @pl.when(z < last)
        def _():
            g_up(r, 0).start()

        g_pair(r, z, 0, k).start()

    def gather_arrive(r, h):
        @pl.when(z + 1 + h <= last)
        def _():
            g_down_in(r, h).wait_recv()
            if h + 1 <= last - 1:
                @pl.when(z > 0)
                def _():
                    g_down(r, h + 1).start()

            g_pair(r, z + 1 + h, 1 + 2 * h, k).start()

        @pl.when(z - 1 - h >= 0)
        def _():
            g_up_in(r, h).wait_recv()
            if h + 1 <= last - 1:
                @pl.when(z < last)
                def _():
                    g_up(r, h + 1).start()

            g_pair(r, z - 1 - h, 2 + 2 * h, k).start()

    def pair_each(r, arr, what):
        what(g_pair(r, z, 0, arr))
        for h in range(last):
            @pl.when(z + 1 + h <= last)
            def _():
                what(g_pair(r, z + 1 + h, 1 + 2 * h, arr))

            @pl.when(z - 1 - h >= 0)
            def _():
                what(g_pair(r, z - 1 - h, 2 + 2 * h, arr))

    def x_pair(r, j):
        return remote(
            px.at[j, span[r]], xch.at[j, span[r]], xs_.at[r, j], xr_.at[r, j], (partner, z)
        )

    def compute(r):
        n = rows[r]
        pair_each(r, 1 - k, lambda c: c.wait_recv())
        hid[0:n, :] = jnp.zeros((n, hid.shape[1]), F32)
        slo[0:n, :] = jnp.zeros((n, slo.shape[1]), F32)

        def into(s, carry):
            cols = pl.ds(pl.multiple_of(s * feat, feat), feat)
            hid[0:n, :] += dot(full[0, s, span[r], :], wv[1, :, cols], (1, 1))
            slo[0:n, :] += dot(full[1, s, span[r], :], wv[0, :, cols], (1, 1))
            return carry

        lax.fori_loop(0, n_ew, into, 0)
        x = hid[0:n, :]
        cdf = 0.5 * (1.0 + lax.erf(x * math.sqrt(0.5)))
        pdf = jnp.exp(-0.5 * x * x) * (1.0 / math.sqrt(2.0 * math.pi))
        hb[0, 0:n, :] = (x * cdf).astype(BF16)
        hb[1, 0:n, :] = (slo[0:n, :] * (cdf + x * pdf)).astype(BF16)

        def other(j, carry):
            cols = pl.ds(pl.multiple_of(j * feat, feat), feat)
            px[j, span[r], :] = dot(hb[1 - k, 0:n, :], wv[1 - k, :, cols]).astype(BF16)
            x_pair(r, j).start()
            return carry

        lax.fori_loop(0, n_ew, other, 0)

        def mine(j, carry):
            cols = pl.ds(pl.multiple_of(j * feat, feat), feat)
            own[j, span[r], :] = dot(hb[k, 0:n, :], wv[k, :, cols]).astype(BF16)
            return carry

        lax.fori_loop(0, n_ew, mine, 0)

    def r_down(r, j, t):
        return remote(sdn.at[j, span[r]], ard.at[j, span[r]], rds.at[r, t], rdr.at[r, t], (me, z - 1))

    def r_up(r, j, t):
        return remote(sup.at[j, span[r]], aru.at[j, span[r]], rus.at[r, t], rur.at[r, t], (me, z + 1))

    def r_down_in(r, j, t):
        return remote(sdn.at[j, span[r]], ard.at[j, span[r]], rds.at[r, t], rdr.at[r, t], (me, z + 1))

    def r_up_in(r, j, t):
        return remote(sup.at[j, span[r]], aru.at[j, span[r]], rus.at[r, t], rur.at[r, t], (me, z - 1))

    def pair_sum(r, j):
        x_pair(r, j).wait_recv()
        return own[j, span[r], :].astype(F32) + xch[j, span[r], :].astype(F32)

    def reduce_step(r, t):
        jd = t - (last - z)

        @pl.when((jd >= 0) & (jd < z))
        def _():
            @pl.when(z == last)
            def _():
                sdn[jd, span[r], :] = pair_sum(r, jd).astype(BF16)

            if t >= 1:
                @pl.when(z < last)
                def _():
                    r_down_in(r, jd, t - 1).wait_recv()
                    sdn[jd, span[r], :] = (
                        pair_sum(r, jd) + ard[jd, span[r], :].astype(F32)
                    ).astype(BF16)

            r_down(r, jd, t).start()

        ju = last - (t - z)

        @pl.when((ju > z) & (ju <= last))
        def _():
            @pl.when(z == 0)
            def _():
                sup[ju, span[r], :] = pair_sum(r, ju).astype(BF16)

            if t >= 1:
                @pl.when(z > 0)
                def _():
                    r_up_in(r, ju, t - 1).wait_recv()
                    sup[ju, span[r], :] = (
                        pair_sum(r, ju) + aru[ju, span[r], :].astype(F32)
                    ).astype(BF16)

            r_up(r, ju, t).start()

    def give_back(r, i):
        d = lax.rem(me + i, n_seq)
        return remote(
            bsend.at[r, d], home.at[k, r, e_me], bs_.at[r, i], br_.at[r, i], (d, z)
        )

    def give_back_in(r, i):
        s = lax.rem(me + n_seq - i, n_seq)
        return remote(
            bsend.at[r, me], home.at[lax.rem(s, 2), r, lax.div(s, 2)],
            bs_.at[r, i], br_.at[r, i], (s, z),
        )

    def finish(r):
        n = rows[r]
        total[0:n, :] = pair_sum(r, z)

        @pl.when(z < last)
        def _():
            r_down_in(r, z, last - 1).wait_recv()
            total[0:n, :] += ard[z, span[r], :].astype(F32)

        @pl.when(z > 0)
        def _():
            r_up_in(r, z, last - 1).wait_recv()
            total[0:n, :] += aru[z, span[r], :].astype(F32)

        term = (gcol[span[r], :] * total[0:n, :]).astype(BF16)
        bsend[r] = dot(uu[span[r], :], term, (0, 0)).astype(BF16).reshape(n_seq, slots, feat)
        for i in range(1, n_seq):
            give_back(r, i).start()
        home[k, r, e_me] = bsend[r, me]

    compact(0)
    gather_start(0)
    compact(1)
    for h in range(last - 1):
        gather_arrive(0, h)
    gather_start(1)
    gather_arrive(0, last - 1)
    for c in w_copies:
        c.wait()
    compute(0)
    for t in range(last):
        gather_arrive(1, t)
        reduce_step(0, t)
    compute(1)
    finish(0)
    for t in range(last):
        reduce_step(1, t)
    finish(1)

    for r in range(2):
        for i in range(1, n_seq):
            give_back_in(r, i).wait_recv()
    sel = pk[...].reshape(2 * experts * slots, tok)
    out_ref[...] = dot(sel, home[0].reshape(2 * experts * slots, feat), (0, 0)).astype(BF16)
    grad_ref[...] = dot(sel, home[1].reshape(2 * experts * slots, feat), (0, 0)).astype(BF16)

    for r in range(2):
        for i in range(1, n_seq):
            dispatch(r, i).wait_send()
            give_back(r, i).wait_send()
        pair_each(r, k, lambda c: c.wait_send())
        for j in range(n_ew):
            x_pair(r, j).wait_send()
        for h in range(last):
            @pl.when((z > 0) & (z + h <= last))
            def _():
                g_down(r, h).wait_send()

            @pl.when((z < last) & (z - h >= 0))
            def _():
                g_up(r, h).wait_send()

            jd = h - (last - z)

            @pl.when((jd >= 0) & (jd < z))
            def _():
                r_down(r, jd, h).wait_send()

            ju = last - (h - z)

            @pl.when((ju > z) & (ju <= last))
            def _():
                r_up(r, ju, h).wait_send()


def per_device(tokens, cotangent, w_in, w_out, bar_picks, gate_weights):
    n_seq = lax.axis_size("seq")
    n_ew = lax.axis_size("ew")
    tok, feat = tokens.shape
    ff, depth = w_in.shape
    experts, cap = bar_picks.shape
    most = max(2, 2 * tok // n_seq)
    slots = -(-((most + 1) // 2) // 16) * 16
    rows = (-(-((cap + n_seq) // 2) // 16) * 16, -(-(cap // 2) // 16) * 16)
    both, top = sum(rows), max(rows)
    dma = pltpu.SemaphoreType.DMA
    vmem = pl.BlockSpec(memory_space=pltpu.VMEM)
    hbm = pl.BlockSpec(memory_space=pl.ANY)
    shape = jax.ShapeDtypeStruct((tok, feat), BF16)
    shards = pltpu.VMEM((n_ew, both, feat), BF16)
    steps = max(1, n_ew - 1)
    return tuple(
        pl.pallas_call(
            functools.partial(kernel, rows, n_seq, n_ew),
            out_shape=(shape, shape),
            in_specs=[vmem, vmem, hbm, hbm, vmem, vmem],
            out_specs=(vmem, vmem),
            scratch_shapes=[
                pltpu.VMEM((2, ff, depth), BF16),
                pltpu.VMEM((2, experts, slots, tok), BF16),
                pltpu.VMEM((both, n_seq * slots), BF16),
                pltpu.VMEM((both, 1), F32),
                pltpu.VMEM((2, 2, experts, slots, feat), BF16),
                pltpu.VMEM((2, n_seq, slots, feat), BF16),
                pltpu.VMEM((2, n_ew, both, feat), BF16),
                pltpu.VMEM((top, ff), F32),
                pltpu.VMEM((top, ff), F32),
                pltpu.VMEM((2, top, ff), BF16),
                shards, shards, shards,
                shards, shards, shards, shards,
                pltpu.VMEM((top, feat), F32),
                pltpu.VMEM((2, n_seq, slots, feat), BF16),
                pltpu.VMEM((2, 2, experts, slots, feat), BF16),
                dma((2,)),
                dma((2, n_seq)), dma((2, n_seq)),
                dma((2, 2 * steps + 1)), dma((2, 2 * steps + 1)),
                dma((2, steps)), dma((2, steps)), dma((2, steps)), dma((2, steps)),
                dma((2, n_ew)), dma((2, n_ew)),
                dma((2, steps)), dma((2, steps)), dma((2, steps)), dma((2, steps)),
                dma((2, n_seq)), dma((2, n_seq)),
            ],
            compiler_params=pltpu.CompilerParams(
                collective_id=0, has_side_effects=True, vmem_limit_bytes=56 * 1024 * 1024
            ),
        )(tokens, cotangent, w_in, w_out, bar_picks, gate_weights)
    )


def solution(mesh):
    in_specs = (
        P("seq", "ew"),
        P("seq", "ew"),
        P(("seq", "ew"), None),
        P(("seq", "ew"), None),
        P(),
        P(),
    )
    out_specs = (P("seq", "ew"), P("seq", "ew"))
    return jax.shard_map(
        per_device, mesh=mesh, in_specs=in_specs, out_specs=out_specs, check_vma=False
    )
```

```python
import functools
import math

import jax
import jax.numpy as jnp
from jax import lax
from jax.experimental import pallas as pl
from jax.experimental.pallas import tpu as pltpu
from jax.sharding import PartitionSpec as P

MESH = pl.DeviceIdType.MESH
F32 = jnp.float32
BF16 = jnp.bfloat16


def iota(shape, dim):
    return lax.broadcasted_iota(jnp.int32, shape, dim).astype(F32)


def columns(*rows):
    fill = jnp.zeros((8 - len(rows), rows[0].shape[1]), F32)
    return jnp.transpose(jnp.concatenate(rows + (fill,), axis=0))


def dot(a, b, dims=(1, 0)):
    return lax.dot_general(
        a, b, (((dims[0],), (dims[1],)), ((), ())), preferred_element_type=F32
    )


def kernel(
    rows, n_seq, n_ew,
    tok_ref, cot_ref, win_ref, wout_ref, picks_ref, gates_ref,
    out_ref, grad_ref,
    wv, pk, uu, gcol, send, recv, full, hid, slo, hb, px, own, xch,
    ard, aru, sdn, sup, total, bsend, home,
    wsem, as_, ar_, ps_, pr_, gds, gdr, gus, gur, xs_, xr_, rds, rdr, rus, rur, bs_, br_,
):
    me = lax.axis_index("seq")
    z = lax.axis_index("ew")
    k = lax.rem(me, 2)
    e_me = lax.div(me, 2)
    partner = me + 1 - 2 * k
    experts, cap = picks_ref.shape
    tok, feat = tok_ref.shape
    slots = send.shape[3]
    starts = [sum(rows[:r]) for r in range(2)]
    last = n_ew - 1
    span = [pl.ds(starts[r], rows[r]) for r in range(2)]
    cut = [-(-rows[r] // 32) * 16 for r in range(2)]
    part = [
        p for r in range(2)
        for p in (pl.ds(starts[r], cut[r]), pl.ds(starts[r] + cut[r], rows[r] - cut[r]))
    ]
    within = [
        p for r in range(2) for p in (pl.ds(0, cut[r]), pl.ds(cut[r], rows[r] - cut[r]))
    ]

    barrier = pltpu.get_barrier_semaphore()
    for i in range(1, n_seq):
        pl.semaphore_signal(
            barrier, inc=1, device_id=(lax.rem(me + i, n_seq), z), device_id_type=MESH
        )

    @pl.when(z > 0)
    def _():
        pl.semaphore_signal(barrier, inc=1, device_id=(me, z - 1), device_id_type=MESH)

    @pl.when(z < last)
    def _():
        pl.semaphore_signal(barrier, inc=1, device_id=(me, z + 1), device_id_type=MESH)

    w_copies = [
        pltpu.make_async_copy(wout_ref, wv.at[0], wsem.at[0]),
        pltpu.make_async_copy(win_ref, wv.at[1], wsem.at[1]),
    ]
    for c in w_copies:
        c.start()

    base = (me * tok).astype(F32)
    local = picks_ref[...].astype(F32) - base
    pad = -experts % 8
    if pad:
        local = jnp.concatenate([local, jnp.full((pad, cap), -1.0, F32)], axis=0)
    local_c = jnp.transpose(local)
    t_row = iota((cap, tok), 1)
    hits = jnp.concatenate(
        [
            jnp.sum(jnp.where(local_c[:, e : e + 1] == t_row, 1.0, 0.0), axis=0, keepdims=True)
            for e in range(experts)
        ]
        + ([jnp.zeros((-experts % 16, tok), F32)] if experts % 16 else []),
        axis=0,
    )
    tri = jnp.where(iota((tok, tok), 0) < iota((tok, tok), 1), 1.0, 0.0).astype(BF16)
    keys = jnp.where(hits > 0.0, dot(hits.astype(BF16), tri), -1.0)
    for r in range(2):
        want = 2.0 * iota((slots, tok), 0) + float(r)
        for e in range(experts):
            pk[r, e] = jnp.where(want == keys[e : e + 1], 1.0, 0.0).astype(BF16)

    inside = (z > 0) & (z < last)

    @pl.when(inside)
    def _():
        pl.semaphore_wait(barrier, n_seq + 1)

    @pl.when(jnp.logical_not(inside))
    def _():
        pl.semaphore_wait(barrier, n_seq)

    def remote(src, dst, s, r, dev):
        return pltpu.make_async_remote_copy(
            src_ref=src, dst_ref=dst, send_sem=s, recv_sem=r, device_id=dev, device_id_type=MESH
        )

    def dispatch(r, i):
        d = lax.rem(me + i, n_seq)
        return remote(
            send.at[r, lax.rem(d, 2), lax.div(d, 2)], recv.at[r, me],
            as_.at[r, i], ar_.at[r, i], (d, z),
        )

    for r in range(2):
        sel = pk[r].reshape(experts * slots, tok)
        send[r, 0] = dot(sel, tok_ref[...]).astype(BF16).reshape(experts, slots, feat)
        send[r, 1] = dot(sel, cot_ref[...]).astype(BF16).reshape(experts, slots, feat)
        for i in range(1, n_seq):
            dispatch(r, i).start()
        recv[r, me] = send[r, k, e_me]

    pick = picks_ref[pl.ds(e_me, 1), :].astype(F32)
    owner = jnp.floor((pick + 0.5) * (1.0 / tok))
    cols = columns(pick, owner)
    rank = jnp.sum(
        jnp.where((cols[:, 1:2] == owner) & (cols[:, 0:1] < pick), 1.0, 0.0),
        axis=0, keepdims=True,
    )
    half = jnp.floor(rank * 0.5)
    cols = columns(owner * float(slots) + half, rank - 2.0 * half, gates_ref[pl.ds(e_me, 1), :])
    slot_c, parity, gate = cols[:, 0:1], cols[:, 1:2], cols[:, 2:3]
    wide = n_seq * slots
    before = jnp.where(iota((wide, wide), 0) < iota((wide, wide), 1), 1.0, 0.0).astype(BF16)
    for r in range(2):
        here = jnp.where(parity == float(r), slot_c, -1.0)
        match = here == iota((cap, wide), 1)
        valid = jnp.sum(jnp.where(match, 1.0, 0.0), axis=0, keepdims=True)
        gate_pad = jnp.sum(jnp.where(match, gate, 0.0), axis=0, keepdims=True)
        place = dot(jnp.broadcast_to(valid, (16, wide)).astype(BF16), before)[0:1]
        place = jnp.where(valid > 0.0, place, -1.0)
        pick_out = iota((rows[r], wide), 0) == place
        uu[span[r], :] = jnp.where(pick_out, 1.0, 0.0).astype(BF16)
        gcol[span[r], :] = jnp.sum(jnp.where(pick_out, gate_pad, 0.0), axis=1, keepdims=True)

    def compact(r):
        for i in range(1, n_seq):
            dispatch(r, i).wait_recv()
        full[k, z, span[r], :] = dot(
            uu[span[r], :], recv[r].reshape(wide, feat)
        ).astype(BF16)

    def g_down(u, h):
        ref = full.at[k, z + h, part[u]]
        return remote(ref, ref, gds.at[u, h], gdr.at[u, h], (me, z - 1))

    def g_up(u, h):
        ref = full.at[k, z - h, part[u]]
        return remote(ref, ref, gus.at[u, h], gur.at[u, h], (me, z + 1))

    def g_down_in(u, h):
        ref = full.at[k, z + 1 + h, part[u]]
        return remote(ref, ref, gds.at[u, h], gdr.at[u, h], (me, z + 1))

    def g_up_in(u, h):
        ref = full.at[k, z - 1 - h, part[u]]
        return remote(ref, ref, gus.at[u, h], gur.at[u, h], (me, z - 1))

    def g_pair(u, s, i, arr):
        ref = full.at[arr, s, part[u]]
        return remote(ref, ref, ps_.at[u, i], pr_.at[u, i], (partner, z))

    def gather_start(r):
        for u in (2 * r, 2 * r + 1):
            @pl.when(z > 0)
            def _():
                g_down(u, 0).start()

            @pl.when(z < last)
            def _():
                g_up(u, 0).start()

            g_pair(u, z, 0, k).start()

    def gather_arrive(r, h):
        for u in (2 * r, 2 * r + 1):
            @pl.when(z + 1 + h <= last)
            def _():
                g_down_in(u, h).wait_recv()
                if h + 1 <= last - 1:
                    @pl.when(z > 0)
                    def _():
                        g_down(u, h + 1).start()

                g_pair(u, z + 1 + h, 1 + 2 * h, k).start()

            @pl.when(z - 1 - h >= 0)
            def _():
                g_up_in(u, h).wait_recv()
                if h + 1 <= last - 1:
                    @pl.when(z < last)
                    def _():
                        g_up(u, h + 1).start()

                g_pair(u, z - 1 - h, 2 + 2 * h, k).start()

    def pair_sent(u):
        g_pair(u, z, 0, k).wait_send()
        for h in range(last):
            @pl.when(z + 1 + h <= last)
            def _():
                g_pair(u, z + 1 + h, 1 + 2 * h, k).wait_send()

            @pl.when(z - 1 - h >= 0)
            def _():
                g_pair(u, z - 1 - h, 2 + 2 * h, k).wait_send()

    def x_pair(r, j):
        return remote(
            px.at[j, span[r]], xch.at[j, span[r]], xs_.at[r, j], xr_.at[r, j], (partner, z)
        )

    def absorb_shard(r, s, i):
        n = rows[r]
        for u in (2 * r, 2 * r + 1):
            g_pair(u, s, i, 1 - k).wait_recv()
        cols = pl.ds(pl.multiple_of(s * feat, feat), feat)
        h_new = dot(full[0, s, span[r], :], wv[1, :, cols], (1, 1))
        s_new = dot(full[1, s, span[r], :], wv[0, :, cols], (1, 1))
        if i == 0:
            hid[0:n, :] = h_new
            slo[0:n, :] = s_new
        else:
            hid[0:n, :] += h_new
            slo[0:n, :] += s_new

    def absorb(r, h):
        if h < 0:
            absorb_shard(r, z, 0)
            return

        @pl.when(z + 1 + h <= last)
        def _():
            absorb_shard(r, z + 1 + h, 1 + 2 * h)

        @pl.when(z - 1 - h >= 0)
        def _():
            absorb_shard(r, z - 1 - h, 2 + 2 * h)

    def activate(r):
        n = rows[r]
        x = hid[0:n, :]
        cdf = 0.5 * (1.0 + lax.erf(x * math.sqrt(0.5)))
        pdf = jnp.exp(-0.5 * x * x) * (1.0 / math.sqrt(2.0 * math.pi))
        hb[0, 0:n, :] = (x * cdf).astype(BF16)
        hb[1, 0:n, :] = (slo[0:n, :] * (cdf + x * pdf)).astype(BF16)

    low = 2 * z < n_ew

    def project(r, i):
        n = rows[r]
        above = last - z
        j_low = jnp.where(i < above, last - i, i - above)
        j_high = jnp.where(i < z, i, last - (i - z))
        j = jnp.where(low, j_low, j_high) if i < last else z
        cols = pl.ds(pl.multiple_of(j * feat, feat), feat)
        px[j, span[r], :] = dot(hb[1 - k, 0:n, :], wv[1 - k, :, cols]).astype(BF16)
        x_pair(r, j).start()
        own[j, span[r], :] = dot(hb[k, 0:n, :], wv[k, :, cols]).astype(BF16)

    def r_down(u, j, t):
        return remote(sdn.at[j, part[u]], ard.at[j, part[u]], rds.at[u, t], rdr.at[u, t], (me, z - 1))

    def r_up(u, j, t):
        return remote(sup.at[j, part[u]], aru.at[j, part[u]], rus.at[u, t], rur.at[u, t], (me, z + 1))

    def r_down_in(u, j, t):
        return remote(sdn.at[j, part[u]], ard.at[j, part[u]], rds.at[u, t], rdr.at[u, t], (me, z + 1))

    def r_up_in(u, j, t):
        return remote(sup.at[j, part[u]], aru.at[j, part[u]], rus.at[u, t], rur.at[u, t], (me, z - 1))

    def pair_sum(u, j):
        return own[j, part[u], :].astype(F32) + xch[j, part[u], :].astype(F32)

    def reduce_step(r, t):
        jd = t - (last - z)

        @pl.when((jd >= 0) & (jd < z))
        def _():
            x_pair(r, jd).wait_recv()
            for u in (2 * r, 2 * r + 1):
                @pl.when(z == last)
                def _():
                    sdn[jd, part[u], :] = pair_sum(u, jd).astype(BF16)

                if t >= 1:
                    @pl.when(z < last)
                    def _():
                        r_down_in(u, jd, t - 1).wait_recv()
                        sdn[jd, part[u], :] = (
                            pair_sum(u, jd) + ard[jd, part[u], :].astype(F32)
                        ).astype(BF16)

                r_down(u, jd, t).start()

        ju = last - (t - z)

        @pl.when((ju > z) & (ju <= last))
        def _():
            x_pair(r, ju).wait_recv()
            for u in (2 * r, 2 * r + 1):
                @pl.when(z == 0)
                def _():
                    sup[ju, part[u], :] = pair_sum(u, ju).astype(BF16)

                if t >= 1:
                    @pl.when(z > 0)
                    def _():
                        r_up_in(u, ju, t - 1).wait_recv()
                        sup[ju, part[u], :] = (
                            pair_sum(u, ju) + aru[ju, part[u], :].astype(F32)
                        ).astype(BF16)

                r_up(u, ju, t).start()

    def give_back(r, i):
        d = lax.rem(me + i, n_seq)
        return remote(
            bsend.at[r, d], home.at[k, r, e_me], bs_.at[r, i], br_.at[r, i], (d, z)
        )

    def give_back_in(r, i):
        s = lax.rem(me + n_seq - i, n_seq)
        return remote(
            bsend.at[r, me], home.at[lax.rem(s, 2), r, lax.div(s, 2)],
            bs_.at[r, i], br_.at[r, i], (s, z),
        )

    def finish(r):
        n = rows[r]
        x_pair(r, z).wait_recv()
        for u in (2 * r, 2 * r + 1):
            total[within[u], :] = pair_sum(u, z)

            @pl.when(z < last)
            def _():
                r_down_in(u, z, last - 1).wait_recv()
                total[within[u], :] += ard[z, part[u], :].astype(F32)

            @pl.when(z > 0)
            def _():
                r_up_in(u, z, last - 1).wait_recv()
                total[within[u], :] += aru[z, part[u], :].astype(F32)

        term = (gcol[span[r], :] * total[0:n, :]).astype(BF16)
        bsend[r] = dot(uu[span[r], :], term, (0, 0)).astype(BF16).reshape(n_seq, slots, feat)
        for i in range(1, n_seq):
            give_back(r, i).start()
        home[k, r, e_me] = bsend[r, me]

    compact(0)
    gather_start(0)
    compact(1)
    for c in w_copies:
        c.wait()
    for h in range(last):
        if h == last - 1:
            gather_start(1)
        gather_arrive(0, h)
        absorb(0, h - 1)
    absorb(0, last - 1)
    activate(0)
    for i in range(last):
        project(0, i)
        gather_arrive(1, i)
        reduce_step(0, i)
        absorb(1, i - 1)
    project(0, last)
    absorb(1, last - 1)
    activate(1)
    for i in range(last):
        project(1, i)
        reduce_step(1, i)
        if i == 0:
            finish(0)
    project(1, last)
    finish(1)

    for r in range(2):
        for i in range(1, n_seq):
            give_back_in(r, i).wait_recv()
    sel = pk[...].reshape(2 * experts * slots, tok)
    out_ref[...] = dot(sel, home[0].reshape(2 * experts * slots, feat), (0, 0)).astype(BF16)
    grad_ref[...] = dot(sel, home[1].reshape(2 * experts * slots, feat), (0, 0)).astype(BF16)

    for r in range(2):
        for i in range(1, n_seq):
            dispatch(r, i).wait_send()
            give_back(r, i).wait_send()
        for j in range(n_ew):
            x_pair(r, j).wait_send()
    for u in range(4):
        pair_sent(u)
        for h in range(last):
            @pl.when((z > 0) & (z + h <= last))
            def _():
                g_down(u, h).wait_send()

            @pl.when((z < last) & (z - h >= 0))
            def _():
                g_up(u, h).wait_send()

            jd = h - (last - z)

            @pl.when((jd >= 0) & (jd < z))
            def _():
                r_down(u, jd, h).wait_send()

            ju = last - (h - z)

            @pl.when((ju > z) & (ju <= last))
            def _():
                r_up(u, ju, h).wait_send()


def per_device(tokens, cotangent, w_in, w_out, bar_picks, gate_weights):
    n_seq = lax.axis_size("seq")
    n_ew = lax.axis_size("ew")
    tok, feat = tokens.shape
    ff, depth = w_in.shape
    experts, cap = bar_picks.shape
    most = max(2, 2 * tok // n_seq)
    slots = -(-((most + 1) // 2) // 16) * 16
    rows = (-(-((cap + n_seq) // 2) // 16) * 16, -(-(cap // 2) // 16) * 16)
    both, top = sum(rows), max(rows)
    dma = pltpu.SemaphoreType.DMA
    vmem = pl.BlockSpec(memory_space=pltpu.VMEM)
    hbm = pl.BlockSpec(memory_space=pl.ANY)
    shape = jax.ShapeDtypeStruct((tok, feat), BF16)
    shards = pltpu.VMEM((n_ew, both, feat), BF16)
    steps = max(1, n_ew - 1)
    return tuple(
        pl.pallas_call(
            functools.partial(kernel, rows, n_seq, n_ew),
            out_shape=(shape, shape),
            in_specs=[vmem, vmem, hbm, hbm, vmem, vmem],
            out_specs=(vmem, vmem),
            scratch_shapes=[
                pltpu.VMEM((2, ff, depth), BF16),
                pltpu.VMEM((2, experts, slots, tok), BF16),
                pltpu.VMEM((both, n_seq * slots), BF16),
                pltpu.VMEM((both, 1), F32),
                pltpu.VMEM((2, 2, experts, slots, feat), BF16),
                pltpu.VMEM((2, n_seq, slots, feat), BF16),
                pltpu.VMEM((2, n_ew, both, feat), BF16),
                pltpu.VMEM((top, ff), F32),
                pltpu.VMEM((top, ff), F32),
                pltpu.VMEM((2, top, ff), BF16),
                shards, shards, shards,
                shards, shards, shards, shards,
                pltpu.VMEM((top, feat), F32),
                pltpu.VMEM((2, n_seq, slots, feat), BF16),
                pltpu.VMEM((2, 2, experts, slots, feat), BF16),
                dma((2,)),
                dma((2, n_seq)), dma((2, n_seq)),
                dma((4, 2 * steps + 1)), dma((4, 2 * steps + 1)),
                dma((4, steps)), dma((4, steps)), dma((4, steps)), dma((4, steps)),
                dma((2, n_ew)), dma((2, n_ew)),
                dma((4, steps)), dma((4, steps)), dma((4, steps)), dma((4, steps)),
                dma((2, n_seq)), dma((2, n_seq)),
            ],
            compiler_params=pltpu.CompilerParams(
                collective_id=0, has_side_effects=True, vmem_limit_bytes=56 * 1024 * 1024
            ),
        )(tokens, cotangent, w_in, w_out, bar_picks, gate_weights)
    )


def solution(mesh):
    in_specs = (
        P("seq", "ew"),
        P("seq", "ew"),
        P(("seq", "ew"), None),
        P(("seq", "ew"), None),
        P(),
        P(),
    )
    out_specs = (P("seq", "ew"), P("seq", "ew"))
    return jax.shard_map(
        per_device, mesh=mesh, in_specs=in_specs, out_specs=out_specs, check_vma=False
    )
```
